512 devices in a mesh: dp: 16 (over y, x), expert: 32 (over z, core).
Axes of the slice: x: 4, y: 4, z: 16, core: 2. Of those that a mesh axis runs over, the one named last changes fastest.
Arguments:
- out_grad: bfloat16 [131072, 2048], P(('dp', 'expert')), may hold values from -6 to 6
- hidden_act: bfloat16 [131072, 2, 768], P(('dp', 'expert')), may hold values from -4 to 4
- expert_ids: int32 [131072, 2], P(('dp', 'expert')), may hold values from 0 to 31, all different within a row; in each aligned block of 256 rows (0 to 255, 256 to 511, ...) at most 32 rows name the same one
- gate_weight: bfloat16 [131072, 2], P(('dp', 'expert')), may hold values from 0.049804688 to 1
- down_weight: bfloat16 [32, 768, 2048], P('expert', 'dp'), may hold values from -0.21875 to 0.21875
- first_moment: float32 [32, 768, 2048], P('expert', 'dp'), may hold values from -12 to 12
- second_moment: float32 [32, 768, 2048], P('expert', 'dp'), may hold values from 0.5 to 8
Outputs:
- hidden_grad: bfloat16 [131072, 2, 768], P(('dp', 'expert'))
- gate_grad: float32 [131072, 2], P(('dp', 'expert'))
- moment_new: float32 [32, 768, 2048], P('expert', 'dp')
- second_new: float32 [32, 768, 2048], P('expert', 'dp')
- update: float32 [32, 768, 2048], P('expert', 'dp')
The draws below stay inside these ranges and needn't reach their ends.
Inputs may be any that keep to these rules, and one draw needn't show every extreme that they name: `expert_ids`: A token's 2 ids differ. Among the slots of one device's 256 tokens, no expert is named more than 32 times, and in every draw some expert is named exactly 32 times by one device's slots.
All inputs are finite; a program needn't handle non-finite values.
Results may differ from the reference program's by a relative error of at most 0.013.
Values may be sent and summed in bfloat16 or wider, within the bound.
A program may use at most 64 MiB of HBM per device.

```python
import math
import jax
import jax.numpy as jnp
import numpy as np
from jax import lax

D = 2048
H = 768
TOP = 2
STEP = 11
TOK_DEV = 256
EXPERTS = 32
MOST = 32
TOKENS = 131072
N_DP = 16
N_EXPERT = 32


def levels(own_key, extent, split, smallest, high):
    factor_of, own = 1.0, jax.random.fold_in(own_key, 6)
    for axis_at, blocks in split:
        heights = jnp.exp(jax.random.uniform(jax.random.fold_in(own, axis_at), (blocks,), jnp.float32, smallest / len(split), high / len(split)))
        factor_of = factor_of * jnp.repeat(heights, extent[axis_at] // blocks).reshape([-1 if axis == axis_at else 1 for axis in range(len(extent))])
    return factor_of


def deal_out(rng, own, number, rows, amount, top, reach, slope):
    sequence = jax.random.permutation(rng, amount)
    packed, usual = portions_of(amount, rows * top, reach, slope, True), portions_of(amount, rows * top, reach, slope, False)
    places = jnp.arange(amount)

    def named(sizes, offset_by):
        used = int((sizes > 0).sum())
        fixed = max(1, used // 4)
        shifted = fixed + (places - fixed + offset_by * (used - fixed)) % max(1, amount - fixed)
        return jnp.zeros((amount,), jnp.int32).at[sequence[jnp.where(places < fixed, places, shifted)]].set(jnp.asarray(sizes, jnp.int32))

    sizes = jnp.where(number % 4 == 0, named(packed, number // 4), named(usual, number - number // 4 - 1))
    mixed = jax.random.permutation(jax.random.fold_in(own, 3), amount)
    giver, taker = mixed[0:amount // 2 * 2:2], mixed[1:amount // 2 * 2:2]
    room = jnp.minimum(sizes[giver] - 1, reach - sizes[taker]) // 2
    room = jnp.where((giver == sequence[0]) | (taker == sequence[0]) | (sizes[taker] == 0), 0, jnp.maximum(room, 0))
    shifted = jax.random.randint(jax.random.fold_in(own, 4), (amount // 2,), 0, 1 << 20) % (room + 1)
    sizes = sizes.at[giver].add(-shifted).at[taker].add(shifted)
    members = jnp.searchsorted(jnp.cumsum(sizes), jnp.arange(rows * top), side="right").astype(jnp.int32)
    listing = members.reshape(top, rows).T
    listing = listing[jax.random.permutation(jax.random.fold_in(own, 1), rows)]
    offset_by = jax.random.randint(jax.random.fold_in(own, 2), (rows, 1), 0, top)
    return jnp.take_along_axis(listing, (jnp.arange(top)[None, :] + offset_by) % top, axis=1)


def portions_of(number_of, total, most, slope, full):
    loads = [(1 << 20) // math.isqrt(rank ** slope) + 1 for rank in range(1, number_of + 1)]
    largest = most if full else min(most, max(-(-total // number_of), total * loads[0] // sum(loads)))
    least = 1 if total - largest >= number_of - 1 else 0
    holding, surplus = [largest] + [least] * (number_of - 1), total - largest - least * (number_of - 1)
    while surplus > 0:
        free = [i for i in range(1, number_of) if holding[i] < largest] or [i for i in range(1, number_of) if holding[i] < most]
        mass, remaining = sum([loads[i] for i in free]), surplus
        for i in free:
            extra = min(most - holding[i], max(1, remaining * loads[i] // mass), surplus)
            holding[i] = holding[i] + extra
            surplus = surplus - extra
    return np.array(holding)


def centred(stream_key, extent, spread, bound, shards=(), kind=jnp.bfloat16):
    values = jax.random.normal(stream_key, extent, jnp.float32) * spread
    if len(shards) > 0:
        values = levels(stream_key, extent, shards, -0.22, 0.18) * values
    return jnp.clip(values, min=-bound, max=bound).astype(kind)


def setup_inputs(seed: int = 0) -> dict:
    keys = jax.random.split(jax.random.key(seed), 8)
    out_grad = centred(keys[0], (TOKENS, D), 1.0, 6.0, ((0, 512),))
    hidden_act = centred(keys[1], (TOKENS, TOP, H), 0.5, 4.0, ((0, 512),))
    expert_ids_keys = jax.random.split(jax.random.fold_in(keys[2], 1), TOKENS // TOK_DEV)
    expert_ids_turns = jax.random.permutation(jax.random.fold_in(keys[2], 3), TOKENS // TOK_DEV)
    expert_ids = jax.vmap(lambda own, number: deal_out(jax.random.fold_in(keys[2], 2), own, number, TOK_DEV, EXPERTS, TOP, MOST, 2))(expert_ids_keys, expert_ids_turns).reshape((TOKENS, TOP))
    gate_weight = jnp.clip(jnp.exp(math.log(1.0) - 2.9996462 * jax.random.uniform(keys[3], (TOKENS, TOP), jnp.float32) ** levels(keys[3], (TOKENS, TOP), ((0, 512),), -0.2, 0.2)), 0.049804688, 1.0).astype(jnp.bfloat16)
    down_weight = centred(keys[4], (EXPERTS, H, D), H ** -0.5, 0.21875, ((0, 32), (1, 16)))
    first_moment = centred(keys[5], (EXPERTS, H, D), 2.0, 12.0, ((0, 32), (1, 16)), jnp.float32)
    second_moment = jnp.clip(jnp.exp(math.log(8.0) - 2.7725887 * jax.random.uniform(keys[6], (EXPERTS, H, D), jnp.float32) ** levels(keys[6], (EXPERTS, H, D), ((0, 32), (1, 16)), -0.2, 0.2)), 0.5, 8.0)
    return {"out_grad": out_grad, "hidden_act": hidden_act, "expert_ids": expert_ids, "gate_weight": gate_weight, "down_weight": down_weight, "first_moment": first_moment, "second_moment": second_moment}


def slot_positions(flat_ids):
    onehot = (flat_ids[:, None] == jnp.arange(EXPERTS, dtype=jnp.int32)[None, :]).astype(jnp.int32)
    running = jnp.cumsum(onehot, axis=0, dtype=jnp.int32)
    return (lax.optimization_barrier(jnp.sum(running * onehot, axis=1, dtype=jnp.int32)) - 1).astype(jnp.int32)

def reference(out_grad, hidden_act, expert_ids, gate_weight, down_weight, first_moment, second_moment):
    block = N_EXPERT * TOK_DEV
    slot_total = N_EXPERT * MOST
    weight_full = down_weight.astype(jnp.float32)

    def one_block(summed, pieces):
        grads, acts, routes, gates = pieces
        per_source = routes.reshape(N_EXPERT, TOK_DEV * TOP)
        position = jax.vmap(slot_positions)(per_source)
        column = (jnp.arange(N_EXPERT, dtype=jnp.int32)[:, None] * MOST + position).reshape(-1).astype(jnp.int32)
        expert_of = per_source.reshape(-1).astype(jnp.int32)
        rows = jnp.repeat(grads, TOP, axis=0)
        gate_flat = gates.reshape(-1, 1).astype(jnp.float32)
        scaled = (gate_flat * rows.astype(jnp.float32)).astype(jnp.bfloat16)
        act_rows = acts.reshape(-1, H)
        grad_buffer = jnp.zeros((EXPERTS, slot_total, D), jnp.bfloat16).at[expert_of, column].set(rows)
        scaled_buffer = jnp.zeros((EXPERTS, slot_total, D), jnp.bfloat16).at[expert_of, column].set(scaled)
        act_buffer = jnp.zeros((EXPERTS, slot_total, H), jnp.bfloat16).at[expert_of, column].set(act_rows)
        partial_value = jnp.einsum('esh,esd->ehd', act_buffer.astype(jnp.float32), scaled_buffer.astype(jnp.float32)).astype(jnp.bfloat16)
        partial_value = lax.optimization_barrier(partial_value)
        reply = jnp.einsum('esd,ehd->esh', grad_buffer.astype(jnp.float32), weight_full).astype(jnp.bfloat16)
        dh_slot = reply[expert_of, column]
        hidden_grad = (gate_flat * dh_slot.astype(jnp.float32)).astype(jnp.bfloat16).reshape(block, TOP, H)
        gate_grad = lax.optimization_barrier(jnp.sum(act_rows.astype(jnp.float32) * dh_slot.astype(jnp.float32), axis=1)).reshape(block, TOP)
        return (summed + partial_value.astype(jnp.float32), (hidden_grad, gate_grad))
    pieces = (out_grad.reshape(N_DP, block, D), hidden_act.reshape(N_DP, block, TOP, H), expert_ids.reshape(N_DP, block, TOP), gate_weight.reshape(N_DP, block, TOP))
    start_sum = jnp.zeros((EXPERTS, H, D), jnp.float32)
    gradient, (hidden_all, gate_all) = lax.scan(one_block, start_sum, pieces)
    hidden_grad = hidden_all.reshape(TOKENS, TOP, H)
    gate_grad = gate_all.reshape(TOKENS, TOP)
    moment_new = 0.9 * first_moment + 0.1 * gradient
    second_new = 0.999 * second_moment + 0.001 * gradient * gradient
    fix_one = 1.0 - 0.9 ** STEP
    fix_two = 1.0 - 0.999 ** STEP
    update = moment_new / fix_one / (jnp.sqrt(second_new / fix_two) + 1e-08)
    return (hidden_grad, gate_grad, moment_new, second_new, update)
```

```python
import functools

import jax
import jax.numpy as jnp
from jax import lax
from jax.experimental import pallas as pl
from jax.experimental.pallas import tpu as pltpu
from jax.sharding import PartitionSpec as P

STEP = 11
MESH = pl.DeviceIdType.MESH
BF = jnp.bfloat16
F32 = jnp.float32

beta_one = 0.9
beta_two = 0.999
adam_eps = 1e-08


def plane_kernel(
    sizes, grads_ref, hid_ref, ids_ref, gate_row_ref, gate_col_ref, w_ref, m_ref, v_ref,
    dh_ref, gg_ref, mo_ref, vo_ref, up_ref,
    s0, s1, send_a, send_g, recv_a, recv_at, recv_g, w_full, part, racc, reply, back,
    stage_r, stage_l, gfin, grecv,
    a_ss, a_rs, g_ss, g_rs, p_ss, p_rs, t_ss, t_rs, gr_ss, gr_rs, gl_ss, gl_rs,
    rr_ss, rr_rs, rl_ss, rl_rs, f_ss, f_rs,
):
    nz, nj, tok, cap, hid, nb, db = sizes
    half = nz // 2
    rows = hid // nz
    slots = nj * cap
    dp = lax.axis_index("dp")
    ez = lax.axis_index("expert")
    z = ez // 2
    core = lax.rem(ez, 2)
    j = dp * 2 + core
    z_up, z_down = lax.rem(z + 1, nz), lax.rem(z + nz - 1, nz)
    up, down, partner = (dp, z_up * 2 + core), (dp, z_down * 2 + core), (z, dp * 2 + core)
    crossed = dp != z

    def peer(i):
        t = lax.rem(j + i, nj)
        return t, (t // 2, z * 2 + lax.rem(t, 2))

    def chunk(t):
        return pl.ds(pl.multiple_of(t * cap, cap), cap)

    def shard(q):
        return pl.ds(pl.multiple_of(q * rows, rows), rows)

    barrier = pltpu.get_barrier_semaphore()

    @pl.loop(1, nj)
    def _(i):
        pl.semaphore_signal(barrier, inc=1, device_id=peer(i)[1], device_id_type=MESH)

    pl.semaphore_signal(barrier, inc=1, device_id=up, device_id_type=MESH)
    pl.semaphore_signal(barrier, inc=1, device_id=down, device_id_type=MESH)

    @pl.when(crossed)
    def _():
        pl.semaphore_signal(barrier, inc=1, device_id=partner, device_id_type=MESH)

    experts = lax.broadcasted_iota(jnp.int32, (nj, tok), 0)
    hot0 = (experts == ids_ref[0:1, :]).astype(F32)
    hot1 = (experts == ids_ref[1:2, :]).astype(F32)
    before = (
        lax.broadcasted_iota(jnp.int32, (tok, tok), 0)
        < lax.broadcasted_iota(jnp.int32, (tok, tok), 1)
    ).astype(F32).astype(BF)
    run0 = jnp.dot(hot0.astype(BF), before, preferred_element_type=F32)
    run1 = jnp.dot(hot1.astype(BF), before, preferred_element_type=F32)
    run1 = run1 + jnp.sum(hot0, axis=1, keepdims=True)
    base = experts.astype(F32) * float(cap)
    place0 = jnp.sum(hot0 * (run0 + base), axis=0, keepdims=True)
    place1 = jnp.sum(hot1 * (run1 + base), axis=0, keepdims=True)
    gate0, gate1 = gate_row_ref[0:1, :], gate_row_ref[1:2, :]
    tile = min(256, slots)

    @pl.loop(0, slots // tile)
    def _(i):
        here = pl.ds(pl.multiple_of(i * tile, tile), tile)
        slot = (lax.broadcasted_iota(jnp.int32, (tile, tok), 0) + i * tile).astype(F32)
        is0 = (slot == place0).astype(F32)
        is1 = (slot == place1).astype(F32)
        s0[here, :] = is0.astype(BF)
        s1[here, :] = is1.astype(BF)
        send_a[here, :] = (
            jnp.dot((is0 * gate0).astype(BF), hid_ref[:, :hid], preferred_element_type=F32)
            + jnp.dot((is1 * gate1).astype(BF), hid_ref[:, hid:], preferred_element_type=F32)
        ).astype(BF)

    pl.semaphore_wait(barrier, nj + 1 + jnp.where(crossed, 1, 0))

    swap = pltpu.make_async_remote_copy(
        src_ref=w_ref, dst_ref=w_full.at[shard(dp), :], send_sem=t_ss, recv_sem=t_rs,
        device_id=partner, device_id_type=MESH,
    )

    @pl.when(crossed)
    def _():
        swap.start()

    @pl.when(jnp.logical_not(crossed))
    def _():
        w_full[shard(z), :] = w_ref[...]

    def act_copy(i):
        t, device = peer(i)
        return pltpu.make_async_remote_copy(
            src_ref=send_a.at[chunk(t), :], dst_ref=recv_a.at[chunk(j), :],
            send_sem=a_ss, recv_sem=a_rs, device_id=device, device_id_type=MESH,
        )

    def grad_copy(i, b):
        t, device = peer(i)
        return pltpu.make_async_remote_copy(
            src_ref=send_g.at[b, chunk(t), :], dst_ref=recv_g.at[b, chunk(j), :],
            send_sem=g_ss.at[b], recv_sem=g_rs.at[b], device_id=device, device_id_type=MESH,
        )

    def reply_copy(i):
        t, device = peer(i)
        return pltpu.make_async_remote_copy(
            src_ref=reply.at[chunk(t), :], dst_ref=back.at[chunk(j), :],
            send_sem=p_ss, recv_sem=p_rs, device_id=device, device_id_type=MESH,
        )

    most = pl.ds(0, slots - cap)

    def wait_rows(ref, sem):
        pltpu.make_async_copy(ref, ref, sem).wait()

    @pl.loop(1, nj)
    def _(i):
        act_copy(i).start()

    recv_a[chunk(j), :] = send_a[chunk(j), :]

    for b in range(nb):

        @pl.loop(0, slots // tile)
        def _(i):
            here = pl.ds(pl.multiple_of(i * tile, tile), tile)
            send_g[b, here, :] = jnp.dot(
                s0[here, :] + s1[here, :], grads_ref[:, b * db : (b + 1) * db], preferred_element_type=F32
            ).astype(BF)

        @pl.loop(1, nj)
        def _(i):
            grad_copy(i, b).start()

        recv_g[b, chunk(j), :] = send_g[b, chunk(j), :]

    def ring_up(s):
        q = shard(lax.rem(z - s + 1 + nz, nz))
        return pltpu.make_async_remote_copy(
            src_ref=w_full.at[q, :], dst_ref=w_full.at[q, :], send_sem=gr_ss.at[s], recv_sem=gr_rs.at[s],
            device_id=up, device_id_type=MESH,
        )

    def ring_down(s):
        q = shard(lax.rem(z + s - 1, nz))
        return pltpu.make_async_remote_copy(
            src_ref=w_full.at[q, :], dst_ref=w_full.at[q, :], send_sem=gl_ss.at[s], recv_sem=gl_rs.at[s],
            device_id=down, device_id_type=MESH,
        )

    @pl.when(crossed)
    def _():
        swap.wait()

    ring_up(1).start()
    ring_down(1).start()

    @pl.loop(1, half)
    def _(s):
        ring_up(s).wait_recv()
        ring_up(s + 1).start()
        ring_down(s).wait_recv()

        @pl.when(s + 1 < half)
        def _():
            ring_down(s + 1).start()

    ring_up(half).wait_recv()

    def sum_up(s, b):
        return pltpu.make_async_remote_copy(
            src_ref=stage_r.at[b, s - 1], dst_ref=stage_r.at[b, s],
            send_sem=rr_ss.at[b, s], recv_sem=rr_rs.at[b, s], device_id=up, device_id_type=MESH,
        )

    def sum_down(s, b):
        return pltpu.make_async_remote_copy(
            src_ref=stage_l.at[b, s - 1], dst_ref=stage_l.at[b, s],
            send_sem=rl_ss.at[b, s], recv_sem=rl_rs.at[b, s], device_id=down, device_id_type=MESH,
        )

    def up_slice(s):
        return shard(lax.rem(z + half - s, nz))

    def down_slice(s):
        return shard(lax.rem(z - half - 1 + s + nz, nz))

    wait_rows(recv_a.at[most, :], a_rs)
    wide = min(256, hid)

    @pl.loop(0, hid // wide)
    def _(i):
        here = pl.ds(pl.multiple_of(i * wide, wide), wide)
        recv_at[here, :] = recv_a[:, here].T

    for b in range(nb):
        wait_rows(recv_g.at[b, most, :], g_rs.at[b])

        @pl.loop(0, hid // wide)
        def _(i):
            here = pl.ds(pl.multiple_of(i * wide, wide), wide)
            part[b, here, :] = jnp.dot(recv_at[here, :], recv_g[b], preferred_element_type=F32)

        stage_r[b, 0] = part[b, up_slice(1), :].astype(BF)
        stage_l[b, 0] = part[b, down_slice(1), :].astype(BF)
        sum_up(1, b).start()
        sum_down(1, b).start()

        @pl.loop(0, slots // tile)
        def _(i):
            here = pl.ds(pl.multiple_of(i * tile, tile), tile)
            product = lax.dot_general(
                recv_g[b, here, :], w_full[:, b * db : (b + 1) * db], (((1,), (1,)), ((), ())),
                preferred_element_type=F32,
            )
            if b == 0:
                racc[here, :] = product
            elif b < nb - 1:
                racc[here, :] += product
            else:
                reply[here, :] = (racc[here, :] + product).astype(BF)

    @pl.loop(1, nj)
    def _(i):
        reply_copy(i).start()

    back[chunk(j), :] = reply[chunk(j), :]

    @pl.loop(1, half)
    def _(s):
        @pl.loop(0, nb)
        def _(b):
            sum_up(s, b).wait_recv()

            @pl.when(s + 1 < half)
            def _():
                stage_r[b, s] = (stage_r[b, s].astype(F32) + part[b, up_slice(s + 1), :]).astype(BF)
                sum_up(s + 1, b).start()

            sum_down(s, b).wait_recv()
            stage_l[b, s] = (stage_l[b, s].astype(F32) + part[b, down_slice(s + 1), :]).astype(BF)
            sum_down(s + 1, b).start()

    def last_copy(b):
        return pltpu.make_async_remote_copy(
            src_ref=gfin.at[b], dst_ref=grecv.at[b], send_sem=f_ss.at[b], recv_sem=f_rs.at[b],
            device_id=partner, device_id_type=MESH,
        )

    @pl.loop(0, nb)
    def _(b):
        sum_down(half, b).wait_recv()
        total = part[b, shard(z), :] + stage_r[b, half - 1].astype(F32) + stage_l[b, half].astype(F32)
        gfin[b] = total.astype(BF)

        @pl.when(crossed)
        def _():
            last_copy(b).start()

        @pl.when(jnp.logical_not(crossed))
        def _():
            grecv[b] = total.astype(BF)

    wait_rows(back.at[most, :], p_rs)
    for k, picks in enumerate((s0, s1)):
        row = lax.dot_general(picks[...], back[...], (((0,), (0,)), ((), ())), preferred_element_type=F32)
        columns = slice(k * hid, (k + 1) * hid)
        dh_ref[:, columns] = (gate_col_ref[:, k : k + 1] * row).astype(BF)
        gg_ref[:, k : k + 1] = jnp.sum(hid_ref[:, columns].astype(F32) * row, axis=1, keepdims=True)

    fix_one = 1.0 - beta_one**STEP
    fix_two = 1.0 - beta_two**STEP
    for b in range(nb):

        @pl.when(crossed)
        def _():
            last_copy(b).wait()

        columns = slice(b * db, (b + 1) * db)
        gradient = grecv[b].astype(F32)
        moment = beta_one * m_ref[:, columns] + (1.0 - beta_one) * gradient
        second = beta_two * v_ref[:, columns] + (1.0 - beta_two) * gradient * gradient
        mo_ref[:, columns] = moment
        vo_ref[:, columns] = second
        up_ref[:, columns] = moment / fix_one / (jnp.sqrt(second / fix_two) + adam_eps)

    wait_rows(send_a.at[most, :], a_ss)
    wait_rows(reply.at[most, :], p_ss)
    for b in range(nb):
        wait_rows(send_g.at[b, most, :], g_ss.at[b])

    @pl.loop(1, half)
    def _(s):
        ring_up(s).wait_send()
        ring_down(s).wait_send()

        @pl.loop(0, nb)
        def _(b):
            sum_up(s, b).wait_send()
            sum_down(s, b).wait_send()

    ring_up(half).wait_send()

    @pl.loop(0, nb)
    def _(b):
        sum_down(half, b).wait_send()


def body(out_grad, hidden_act, expert_ids, gate_weight, down_weight, first_moment, second_moment):
    tok, top = expert_ids.shape
    width = out_grad.shape[1]
    hid = hidden_act.shape[2]
    nz = lax.axis_size("expert") // 2
    nj = 2 * lax.axis_size("dp")
    cap = 2 * tok * top // nj
    slots = nj * cap
    rows = hid // nz
    half = nz // 2
    nb = 4
    db = width // nb
    gate = gate_weight.astype(F32)
    dma = pltpu.SemaphoreType.DMA
    vmem = pl.BlockSpec(memory_space=pltpu.VMEM)
    dh, gg, mo, vo, up = pl.pallas_call(
        functools.partial(plane_kernel, (nz, nj, tok, cap, hid, nb, db)),
        out_shape=(
            jax.ShapeDtypeStruct((tok, top * hid), BF),
            jax.ShapeDtypeStruct((tok, top), F32),
            jax.ShapeDtypeStruct((rows, width), F32),
            jax.ShapeDtypeStruct((rows, width), F32),
            jax.ShapeDtypeStruct((rows, width), F32),
        ),
        in_specs=[vmem] * 8,
        out_specs=(vmem,) * 5,
        scratch_shapes=[
            pltpu.VMEM((slots, tok), BF),
            pltpu.VMEM((slots, tok), BF),
            pltpu.VMEM((slots, hid), BF),
            pltpu.VMEM((nb, slots, db), BF),
            pltpu.VMEM((slots, hid), BF),
            pltpu.VMEM((hid, slots), BF),
            pltpu.VMEM((nb, slots, db), BF),
            pltpu.VMEM((hid, width), BF),
            pltpu.VMEM((nb, hid, db), F32),
            pltpu.VMEM((slots, hid), F32),
            pltpu.VMEM((slots, hid), BF),
            pltpu.VMEM((slots, hid), BF),
            pltpu.VMEM((nb, half, rows, db), BF),
            pltpu.VMEM((nb, half + 1, rows, db), BF),
            pltpu.VMEM((nb, rows, db), BF),
            pltpu.VMEM((nb, rows, db), BF),
            dma, dma, dma((nb,)), dma((nb,)), dma, dma, dma, dma,
            dma((half + 1,)), dma((half + 1,)), dma((half + 1,)), dma((half + 1,)),
            dma((nb, half + 1)), dma((nb, half + 1)), dma((nb, half + 1)), dma((nb, half + 1)),
            dma((nb,)), dma((nb,)),
        ],
        compiler_params=pltpu.CompilerParams(
            collective_id=0, has_side_effects=True, vmem_limit_bytes=58 * 1024 * 1024
        ),
    )(
        out_grad, hidden_act.reshape(tok, top * hid), expert_ids.T, gate.T, gate,
        down_weight[0], first_moment[0], second_moment[0],
    )
    return dh.reshape(tok, top, hid), gg, mo[None], vo[None], up[None]


def solution(mesh):
    return jax.shard_map(
        body,
        mesh=mesh,
        in_specs=(
            P(("dp", "expert"), None),
            P(("dp", "expert"), None, None),
            P(("dp", "expert"), None),
            P(("dp", "expert"), None),
            P("expert", "dp", None),
            P("expert", "dp", None),
            P("expert", "dp", None),
        ),
        out_specs=(
            P(("dp", "expert"), None, None),
            P(("dp", "expert"), None),
            P("expert", "dp", None),
            P("expert", "dp", None),
            P("expert", "dp", None),
        ),
        check_vma=False,
    )
```

```python
import functools

import jax
import jax.numpy as jnp
from jax import lax
from jax.experimental import pallas as pl
from jax.experimental.pallas import tpu as pltpu
from jax.sharding import PartitionSpec as P

STEP = 11
MESH = pl.DeviceIdType.MESH
BF = jnp.bfloat16
F32 = jnp.float32

beta_one = 0.9
beta_two = 0.999
adam_eps = 1e-08


def plane_kernel(
    sizes, grads_ref, hid_ref, ids_ref, gate_ref, w_ref,
    dh_ref, gg_ref, grad_ref,
    pick, flat_pick, send_a, send_g, recv_a, recv_at, recv_g, w_full, part, reply, back,
    stage_r, stage_l, gfin, w_half, g_half,
    a_ss, a_rs, g_ss, g_rs, p_ss, p_rs, t_ss, t_rs, u_ss, u_rs, gr_ss, gr_rs, gl_ss, gl_rs,
    rr_ss, rr_rs, rl_ss, rl_rs, f_ss, f_rs, h_ss, h_rs,
):
    nz, nj, tok, cap, hid, nb, db, pieces = sizes
    half = nz // 2
    rows = hid // nz
    thin = rows // pieces
    slots = nj * cap
    own = 2 * tok
    dp = lax.axis_index("dp")
    ez = lax.axis_index("expert")
    z = ez // 2
    core = lax.rem(ez, 2)
    j = dp * 2 + core
    z_up, z_down = lax.rem(z + 1, nz), lax.rem(z + nz - 1, nz)
    up, down = (dp, z_up * 2 + core), (dp, z_down * 2 + core)

    def lag(k):
        return k * nz // pieces

    def mirrored(k):
        return lax.rem(dp + lag(k) - z + nz, nz)

    def entered(k, q):
        return lax.rem(dp + q - lag(k) + 2 * nz, nz)

    def peer(i):
        if nj != 32:
            t = lax.rem(j + i + 1, nj)
            return t, (t // 2, z * 2 + lax.rem(t, 2))
        turn = lax.rem(i, 4)
        cos = (1 - turn) * (1 - lax.rem(turn, 2))
        sin = (2 - turn) * lax.rem(turn, 2)
        reach = lax.rem(i // 4, 3)
        early = i < 24
        rest = 3 - turn
        dy = jnp.where(early, reach * cos + sin, 2 * (rest // 2))
        dx = jnp.where(early, cos - reach * sin, 2 * lax.rem(rest, 2))
        dc = jnp.where(early, 1 - i // 12, 1 - (i - 24) // 4)
        mirror = 1 - 2 * core
        y = lax.rem(dp // 4 + mirror * dy + 4, 4)
        x = lax.rem(lax.rem(dp, 4) + mirror * dx + 4, 4)
        c = lax.rem(core + dc, 2)
        return (y * 4 + x) * 2 + c, (y * 4 + x, z * 2 + c)

    def chunk(t):
        return pl.ds(pl.multiple_of(t * cap, cap), cap)

    def shard(q):
        return pl.ds(pl.multiple_of(q * rows, rows), rows)

    barrier = pltpu.get_barrier_semaphore()

    @pl.loop(0, nj - 1)
    def _(i):
        pl.semaphore_signal(barrier, inc=1, device_id=peer(i)[1], device_id_type=MESH)

    pl.semaphore_signal(barrier, inc=1, device_id=up, device_id_type=MESH)
    pl.semaphore_signal(barrier, inc=1, device_id=down, device_id_type=MESH)

    for k in range(pieces):

        @pl.when(mirrored(k) != z)
        def _():
            across = (dp, mirrored(k) * 2 + core)
            pl.semaphore_signal(barrier, inc=1, device_id=across, device_id_type=MESH)

    experts = lax.broadcasted_iota(jnp.int32, (nj, tok), 0)
    hot0 = (experts == ids_ref[0:1, :]).astype(F32)
    hot1 = (experts == ids_ref[1:2, :]).astype(F32)
    before = (
        lax.broadcasted_iota(jnp.int32, (tok, tok), 0)
        < lax.broadcasted_iota(jnp.int32, (tok, tok), 1)
    ).astype(F32).astype(BF)
    run0 = jnp.dot(hot0.astype(BF), before, preferred_element_type=F32)
    run1 = jnp.dot(hot1.astype(BF), before, preferred_element_type=F32)
    run1 = run1 + jnp.sum(hot0, axis=1, keepdims=True)
    rank0 = jnp.sum(hot0 * run0, axis=0, keepdims=True)
    rank1 = jnp.sum(hot1 * run1, axis=0, keepdims=True)
    place0 = ids_ref[0:1, :].astype(F32) * float(cap) + rank0
    place1 = ids_ref[1:2, :].astype(F32) * float(cap) + rank1
    blank = jnp.zeros((5, tok), F32)
    token = lax.broadcasted_iota(jnp.int32, (tok, own), 0) * 2
    slot = lax.broadcasted_iota(jnp.int32, (tok, own), 1)
    flat = jnp.zeros((8, own), F32)
    for k, rank in enumerate((rank0, rank1)):
        facts = jnp.concatenate(
            [ids_ref[k : k + 1, :].astype(F32), rank, gate_ref[k : k + 1, :].astype(F32), blank], axis=0
        )
        spread = (slot == token + k).astype(F32).astype(BF)
        flat = flat + jnp.dot(facts.astype(BF), spread, preferred_element_type=F32)
    place = flat[0:1, :] * float(cap) + flat[1:2, :]
    gate = flat[2:3, :]
    gate_col = flat.T[:, 2:3]
    tile = min(256, slots)

    pl.semaphore_wait(barrier, nj + 1 + sum(jnp.where(mirrored(k) != z, 1, 0) for k in range(pieces)))

    def piece(k):
        return pl.ds(pl.multiple_of(k * thin, thin), thin)

    def placed(p, k):
        return pl.ds(pl.multiple_of(p * rows + k * thin, thin), thin)

    def fold_copy(k):
        return pltpu.make_async_remote_copy(
            src_ref=w_ref.at[piece(k), :], dst_ref=w_half.at[k], send_sem=t_ss.at[k], recv_sem=t_rs.at[k],
            device_id=(dp, mirrored(k) * 2 + core), device_id_type=MESH,
        )

    def enter_copy(k):
        return pltpu.make_async_remote_copy(
            src_ref=w_half.at[k], dst_ref=w_full.at[placed(dp, k), :], send_sem=u_ss.at[k], recv_sem=u_rs.at[k],
            device_id=(mirrored(k), z * 2 + core), device_id_type=MESH,
        )

    @pl.loop(0, pieces)
    def _(k):
        @pl.when(mirrored(k) != z)
        def _():
            fold_copy(k).start()

        @pl.when(mirrored(k) == z)
        def _():
            w_half[k] = w_ref[piece(k), :]

    @pl.loop(0, slots // tile)
    def _(i):
        here = pl.ds(pl.multiple_of(i * tile, tile), tile)
        slot = (lax.broadcasted_iota(jnp.int32, (tile, tok), 0) + i * tile).astype(F32)
        pick[here, :] = ((slot == place0).astype(F32) + (slot == place1).astype(F32)).astype(BF)
        slot = (lax.broadcasted_iota(jnp.int32, (tile, own), 0) + i * tile).astype(F32)
        chosen = (slot == place).astype(F32)
        flat_pick[here, :] = chosen.astype(BF)
        send_a[here, :] = jnp.dot(
            (chosen * gate).astype(BF), hid_ref[...], preferred_element_type=F32
        ).astype(BF)

    def act_copy(i):
        t, device = peer(i)
        return pltpu.make_async_remote_copy(
            src_ref=send_a.at[chunk(t), :], dst_ref=recv_a.at[chunk(j), :],
            send_sem=a_ss, recv_sem=a_rs, device_id=device, device_id_type=MESH,
        )

    def grad_copy(i, b):
        t, device = peer(i)
        return pltpu.make_async_remote_copy(
            src_ref=send_g.at[b, chunk(t), :], dst_ref=recv_g.at[b, chunk(j), :],
            send_sem=g_ss.at[b], recv_sem=g_rs.at[b], device_id=device, device_id_type=MESH,
        )

    def reply_copy(i):
        t, device = peer(i)
        return pltpu.make_async_remote_copy(
            src_ref=reply.at[chunk(t), :], dst_ref=back.at[chunk(j), :],
            send_sem=p_ss, recv_sem=p_rs, device_id=device, device_id_type=MESH,
        )

    most = pl.ds(0, slots - cap)

    def wait_rows(ref, sem):
        pltpu.make_async_copy(ref, ref, sem).wait()

    @pl.loop(0, nj - 1)
    def _(i):
        act_copy(i).start()

    recv_a[chunk(j), :] = send_a[chunk(j), :]

    def send_block(b):
        @pl.loop(0, slots // tile)
        def _(i):
            here = pl.ds(pl.multiple_of(i * tile, tile), tile)
            send_g[b, here, :] = jnp.dot(
                pick[here, :], grads_ref[:, b * db : (b + 1) * db], preferred_element_type=F32
            ).astype(BF)

        @pl.loop(0, nj - 1)
        def _(i):
            grad_copy(i, b).start()

        recv_g[b, chunk(j), :] = send_g[b, chunk(j), :]

    def ring_up(s, k):
        q = placed(entered(k, lax.rem(z - s + 1 + nz, nz)), k)
        return pltpu.make_async_remote_copy(
            src_ref=w_full.at[q, :], dst_ref=w_full.at[q, :], send_sem=gr_ss.at[s, k], recv_sem=gr_rs.at[s, k],
            device_id=up, device_id_type=MESH,
        )

    def ring_down(s, k):
        q = placed(entered(k, lax.rem(z + s - 1, nz)), k)
        return pltpu.make_async_remote_copy(
            src_ref=w_full.at[q, :], dst_ref=w_full.at[q, :], send_sem=gl_ss.at[s, k], recv_sem=gl_rs.at[s, k],
            device_id=down, device_id_type=MESH,
        )

    def gather_enter():
        @pl.loop(0, pieces)
        def _(k):
            @pl.when(mirrored(k) != z)
            def _():
                fold_copy(k).wait()

            @pl.when(mirrored(k) != dp)
            def _():
                enter_copy(k).start()

            @pl.when(mirrored(k) == dp)
            def _():
                w_full[placed(dp, k), :] = w_half[k]

    def gather_begin():
        @pl.loop(0, pieces)
        def _(k):
            @pl.when(mirrored(k) != dp)
            def _():
                enter_copy(k).wait()

            ring_up(1, k).start()
            if half > 1:
                ring_down(1, k).start()

    def gather_steps(first, last):
        @pl.loop(first, min(last, half - 1) + 1)
        def _(s):
            @pl.loop(0, pieces)
            def _(k):
                ring_up(s, k).wait_recv()
                ring_up(s + 1, k).start()
                ring_down(s, k).wait_recv()

                @pl.when(s + 1 < half)
                def _():
                    ring_down(s + 1, k).start()

        if last >= half:

            @pl.loop(0, pieces)
            def _(k):
                ring_up(half, k).wait_recv()

    def sum_up(s, b):
        return pltpu.make_async_remote_copy(
            src_ref=stage_r.at[b, s - 1], dst_ref=stage_r.at[b, s],
            send_sem=rr_ss.at[b, s], recv_sem=rr_rs.at[b, s], device_id=up, device_id_type=MESH,
        )

    def sum_down(s, b):
        return pltpu.make_async_remote_copy(
            src_ref=stage_l.at[b, s - 1], dst_ref=stage_l.at[b, s],
            send_sem=rl_ss.at[b, s], recv_sem=rl_rs.at[b, s], device_id=down, device_id_type=MESH,
        )

    def up_slice(s):
        return shard(lax.rem(z + half - s, nz))

    def down_slice(s):
        return shard(lax.rem(z - half - 1 + s + nz, nz))

    def leave_copy(b, k):
        return pltpu.make_async_remote_copy(
            src_ref=gfin.at[b, piece(k), :], dst_ref=g_half.at[b, k], send_sem=f_ss.at[b, k], recv_sem=f_rs.at[b, k],
            device_id=(entered(k, z), z * 2 + core), device_id_type=MESH,
        )

    def home_copy(b, k):
        return pltpu.make_async_remote_copy(
            src_ref=g_half.at[b, k], dst_ref=grad_ref.at[piece(k), b * db : (b + 1) * db],
            send_sem=h_ss.at[b, k], recv_sem=h_rs.at[b, k],
            device_id=(dp, mirrored(k) * 2 + core), device_id_type=MESH,
        )

    def home(b):
        @pl.loop(0, pieces)
        def _(k):
            @pl.when(entered(k, z) != dp)
            def _():
                leave_copy(b, k).wait()

            @pl.when(mirrored(k) != z)
            def _():
                home_copy(b, k).start()

            @pl.when(mirrored(k) == z)
            def _():
                grad_ref[piece(k), b * db : (b + 1) * db] = g_half[b, k]

    following = {}

    def sum_begin(b):
        stage_l[b, 0] = part[b, down_slice(1), :].astype(BF)
        sum_down(1, b).start()
        if half > 1:
            stage_r[b, 0] = part[b, up_slice(1), :].astype(BF)
            sum_up(1, b).start()
        following[b] = 1

    def sum_end(b):
        sum_down(half, b).wait_recv()
        total = part[b, shard(z), :] + stage_r[b, half - 1].astype(F32) + stage_l[b, half].astype(F32)
        gfin[b] = total.astype(BF)

        @pl.loop(0, pieces)
        def _(k):
            @pl.when(entered(k, z) != dp)
            def _():
                leave_copy(b, k).start()

            @pl.when(entered(k, z) == dp)
            def _():
                g_half[b, k] = gfin[b, piece(k), :]

        if b > 0:
            home(b - 1)

    def sum_steps(count):
        while count and following:
            n = min([count] + [half - s for s in following.values()])

            @pl.loop(0, n)
            def _(i):
                for b, first in following.items():
                    s = first + i
                    sum_down(s, b).wait_recv()
                    stage_l[b, s] = (stage_l[b, s].astype(F32) + part[b, down_slice(s + 1), :]).astype(BF)
                    sum_down(s + 1, b).start()
                    sum_up(s, b).wait_recv()

                    @pl.when(s + 1 < half)
                    def _():
                        stage_r[b, s] = (stage_r[b, s].astype(F32) + part[b, up_slice(s + 1), :]).astype(BF)
                        sum_up(s + 1, b).start()

            for b in list(following):
                following[b] += n
                if following[b] == half:
                    del following[b]
                    sum_end(b)
            count -= n

    wide = min(256, hid)

    def turn_acts():
        wait_rows(recv_a.at[most, :], a_rs)

        @pl.loop(0, hid // wide)
        def _(i):
            here = pl.ds(pl.multiple_of(i * wide, wide), wide)
            turned = recv_a[:, here].T
            for u in range(wide // thin):
                block = i * (wide // thin) + u
                k = lax.rem(block, pieces)
                q = lax.rem(block // pieces - dp + lag(k) + nz, nz)
                recv_at[placed(q, k), :] = turned[u * thin : (u + 1) * thin, :]

    def sum_block(b):
        wait_rows(recv_g.at[b, most, :], g_rs.at[b])

        @pl.loop(0, hid // wide)
        def _(i):
            here = pl.ds(pl.multiple_of(i * wide, wide), wide)
            part[b, here, :] = jnp.dot(recv_at[here, :], recv_g[b], preferred_element_type=F32)

        sum_begin(b)

    def reply_rows(i):
        here = slice(i * tile, (i + 1) * tile)
        reply[here, :] = sum(
            lax.dot_general(
                recv_g[b, here, :], w_full[:, b * db : (b + 1) * db], (((1,), (1,)), ((), ())),
                preferred_element_type=F32,
            )
            for b in range(nb)
        ).astype(BF)

    def gather_step(s):
        if s <= half:
            gather_steps(s, s)

    send_block(0)
    gather_enter()
    send_block(1)
    gather_begin()
    send_block(2)
    gather_step(1)
    send_block(3)
    gather_step(2)
    gather_step(3)
    turn_acts()
    sum_block(0)
    gather_step(4)
    sum_steps(1)
    gather_step(5)
    sum_steps(1)
    sum_block(1)
    gather_step(6)
    sum_steps(1)
    gather_step(7)
    sum_steps(1)
    sum_block(2)
    gather_step(8)
    sum_steps(2)
    sum_block(3)
    for i in range(slots // tile):
        reply_rows(i)
        sum_steps(1)

    @pl.loop(0, nj - 1)
    def _(i):
        reply_copy(i).start()

    back[chunk(j), :] = reply[chunk(j), :]
    sum_steps(half * nb)
    home(nb - 1)

    wait_rows(back.at[most, :], p_rs)
    row = lax.dot_general(flat_pick[...], back[...], (((0,), (0,)), ((), ())), preferred_element_type=F32)
    dh_ref[...] = (gate_col * row).astype(BF)
    sums = jnp.sum(hid_ref[...].astype(F32) * row, axis=1, keepdims=True)
    token = lax.broadcasted_iota(jnp.int32, (own, tok), 1) * 2
    slot = lax.broadcasted_iota(jnp.int32, (own, tok), 0)
    for k in range(2):
        gg_ref[k : k + 1, :] = jnp.sum(jnp.where(slot == token + k, sums, 0.0), axis=0, keepdims=True)

    wait_rows(send_a.at[most, :], a_ss)
    wait_rows(reply.at[most, :], p_ss)
    for b in range(nb):
        wait_rows(send_g.at[b, most, :], g_ss.at[b])

    @pl.loop(1, half)
    def _(s):
        @pl.loop(0, pieces)
        def _(k):
            ring_up(s, k).wait_send()
            ring_down(s, k).wait_send()

        @pl.loop(0, nb)
        def _(b):
            sum_up(s, b).wait_send()
            sum_down(s, b).wait_send()

    @pl.loop(0, pieces)
    def _(k):
        ring_up(half, k).wait_send()

    @pl.loop(0, nb)
    def _(b):
        sum_down(half, b).wait_send()

    for b in range(nb):

        @pl.loop(0, pieces)
        def _(k):
            @pl.when(mirrored(k) != z)
            def _():
                home_copy(b, k).wait()


def body(out_grad, hidden_act, expert_ids, gate_weight, down_weight, first_moment, second_moment):
    tok, top = expert_ids.shape
    width = out_grad.shape[1]
    hid = hidden_act.shape[2]
    nz = lax.axis_size("expert") // 2
    nj = 2 * lax.axis_size("dp")
    cap = 2 * tok * top // nj
    slots = nj * cap
    own = tok * top
    rows = hid // nz
    half = nz // 2
    nb = 4
    db = width // nb
    pieces = rows // 16
    dma = pltpu.SemaphoreType.DMA
    vmem = pl.BlockSpec(memory_space=pltpu.VMEM)
    dh, gg, gradient = pl.pallas_call(
        functools.partial(plane_kernel, (nz, nj, tok, cap, hid, nb, db, pieces)),
        out_shape=(
            jax.ShapeDtypeStruct((own, hid), BF),
            jax.ShapeDtypeStruct((top, tok), F32),
            jax.ShapeDtypeStruct((rows, width), BF),
        ),
        in_specs=[vmem] * 5,
        out_specs=(vmem,) * 3,
        scratch_shapes=[
            pltpu.VMEM((slots, tok), BF),
            pltpu.VMEM((slots, own), BF),
            pltpu.VMEM((slots, hid), BF),
            pltpu.VMEM((nb, slots, db), BF),
            pltpu.VMEM((slots, hid), BF),
            pltpu.VMEM((hid, slots), BF),
            pltpu.VMEM((nb, slots, db), BF),
            pltpu.VMEM((hid, width), BF),
            pltpu.VMEM((nb, hid, db), F32),
            pltpu.VMEM((slots, hid), BF),
            pltpu.VMEM((slots, hid), BF),
            pltpu.VMEM((nb, half, rows, db), BF),
            pltpu.VMEM((nb, half + 1, rows, db), BF),
            pltpu.VMEM((nb, rows, db), BF),
            pltpu.VMEM((pieces, rows // pieces, width), BF),
            pltpu.VMEM((nb, pieces, rows // pieces, db), BF),
            dma, dma, dma((nb,)), dma((nb,)), dma, dma,
            dma((pieces,)), dma((pieces,)), dma((pieces,)), dma((pieces,)),
            dma((half + 1, pieces)), dma((half + 1, pieces)), dma((half + 1, pieces)), dma((half + 1, pieces)),
            dma((nb, half + 1)), dma((nb, half + 1)), dma((nb, half + 1)), dma((nb, half + 1)),
            dma((nb, pieces)), dma((nb, pieces)), dma((nb, pieces)), dma((nb, pieces)),
        ],
        compiler_params=pltpu.CompilerParams(
            collective_id=0, has_side_effects=True, vmem_limit_bytes=58 * 1024 * 1024
        ),
    )(
        out_grad, hidden_act.reshape(own, hid), expert_ids.T, gate_weight.T, down_weight[0],
    )
    gradient = gradient.astype(F32)
    moment_new = beta_one * first_moment[0] + (1.0 - beta_one) * gradient
    second_new = beta_two * second_moment[0] + (1.0 - beta_two) * gradient * gradient
    fix_one = 1.0 - beta_one**STEP
    fix_two = 1.0 - beta_two**STEP
    update = moment_new / fix_one / (jnp.sqrt(second_new / fix_two) + adam_eps)
    return dh.reshape(tok, top, hid), gg.T, moment_new[None], second_new[None], update[None]


def solution(mesh):
    return jax.shard_map(
        body,
        mesh=mesh,
        in_specs=(
            P(("dp", "expert"), None),
            P(("dp", "expert"), None, None),
            P(("dp", "expert"), None),
            P(("dp", "expert"), None),
            P("expert", "dp", None),
            P("expert", "dp", None),
            P("expert", "dp", None),
        ),
        out_specs=(
            P(("dp", "expert"), None, None),
            P(("dp", "expert"), None),
            P("expert", "dp", None),
            P("expert", "dp", None),
            P("expert", "dp", None),
        ),
        check_vma=False,
    )
```

```python
import functools

import jax
import jax.numpy as jnp
from jax import lax
from jax.experimental import pallas as pl
from jax.experimental.pallas import tpu as pltpu
from jax.sharding import PartitionSpec as P

STEP = 11
MESH = pl.DeviceIdType.MESH
BF = jnp.bfloat16
F32 = jnp.float32

beta_one = 0.9
beta_two = 0.999
adam_eps = 1e-08


def plane_kernel(
    sizes, grads_ref, hid_ref, ids_ref, gate_ref, w_ref,
    dh_ref, gg_ref, grad_ref,
    pick, flat_pick, send_a, send_g, recv_a, recv_at, recv_g, w_full, part, reply, back,
    stage_r, stage_l, gfin, w_half, g_half,
    a_ss, a_rs, g_ss, g_rs, p_ss, p_rs, t_ss, t_rs, u_ss, u_rs, gr_ss, gr_rs, gl_ss, gl_rs,
    rr_ss, rr_rs, rl_ss, rl_rs, f_ss, f_rs, h_ss, h_rs,
):
    nz, nj, tok, cap, hid, nb, db, pieces = sizes
    half = nz // 2
    rows = hid // nz
    thin = rows // pieces
    slots = nj * cap
    own = 2 * tok
    dp = lax.axis_index("dp")
    ez = lax.axis_index("expert")
    z = ez // 2
    core = lax.rem(ez, 2)
    j = dp * 2 + core
    z_up, z_down = lax.rem(z + 1, nz), lax.rem(z + nz - 1, nz)
    up, down = (dp, z_up * 2 + core), (dp, z_down * 2 + core)

    def lag(k):
        return k * nz // pieces

    def mirrored(k):
        return lax.rem(dp + lag(k) - z + nz, nz)

    def entered(k, q):
        return lax.rem(dp + q - lag(k) + 2 * nz, nz)

    def peer(i):
        if nj != 32:
            t = lax.rem(j + i + 1, nj)
            return t, (t // 2, z * 2 + lax.rem(t, 2))
        turn = lax.rem(i, 4)
        cos = (1 - turn) * (1 - lax.rem(turn, 2))
        sin = (2 - turn) * lax.rem(turn, 2)
        reach = lax.rem(i // 4, 3)
        early = i < 24
        rest = 3 - turn
        dy = jnp.where(early, reach * cos + sin, 2 * (rest // 2))
        dx = jnp.where(early, cos - reach * sin, 2 * lax.rem(rest, 2))
        dc = jnp.where(early, 1 - i // 12, 1 - (i - 24) // 4)
        mirror = 1 - 2 * core
        y = lax.rem(dp // 4 + mirror * dy + 4, 4)
        x = lax.rem(lax.rem(dp, 4) + mirror * dx + 4, 4)
        c = lax.rem(core + dc, 2)
        return (y * 4 + x) * 2 + c, (y * 4 + x, z * 2 + c)

    def chunk(t):
        return pl.ds(pl.multiple_of(t * cap, cap), cap)

    def shard(q):
        return pl.ds(pl.multiple_of(q * rows, rows), rows)

    barrier = pltpu.get_barrier_semaphore()

    @pl.loop(0, nj - 1)
    def _(i):
        pl.semaphore_signal(barrier, inc=1, device_id=peer(i)[1], device_id_type=MESH)

    pl.semaphore_signal(barrier, inc=1, device_id=up, device_id_type=MESH)
    pl.semaphore_signal(barrier, inc=1, device_id=down, device_id_type=MESH)

    for k in range(pieces):

        @pl.when(mirrored(k) != z)
        def _():
            across = (dp, mirrored(k) * 2 + core)
            pl.semaphore_signal(barrier, inc=1, device_id=across, device_id_type=MESH)

    experts = lax.broadcasted_iota(jnp.int32, (nj, tok), 0)
    hot0 = (experts == ids_ref[0:1, :]).astype(F32)
    hot1 = (experts == ids_ref[1:2, :]).astype(F32)
    before = (
        lax.broadcasted_iota(jnp.int32, (tok, tok), 0)
        < lax.broadcasted_iota(jnp.int32, (tok, tok), 1)
    ).astype(F32).astype(BF)
    run0 = jnp.dot(hot0.astype(BF), before, preferred_element_type=F32)
    run1 = jnp.dot(hot1.astype(BF), before, preferred_element_type=F32)
    run1 = run1 + jnp.sum(hot0, axis=1, keepdims=True)
    rank0 = jnp.sum(hot0 * run0, axis=0, keepdims=True)
    rank1 = jnp.sum(hot1 * run1, axis=0, keepdims=True)
    place0 = ids_ref[0:1, :].astype(F32) * float(cap) + rank0
    place1 = ids_ref[1:2, :].astype(F32) * float(cap) + rank1
    blank = jnp.zeros((5, tok), F32)
    token = lax.broadcasted_iota(jnp.int32, (tok, own), 0) * 2
    slot = lax.broadcasted_iota(jnp.int32, (tok, own), 1)
    flat = jnp.zeros((8, own), F32)
    for k, rank in enumerate((rank0, rank1)):
        facts = jnp.concatenate(
            [ids_ref[k : k + 1, :].astype(F32), rank, gate_ref[k : k + 1, :].astype(F32), blank], axis=0
        )
        spread = (slot == token + k).astype(F32).astype(BF)
        flat = flat + jnp.dot(facts.astype(BF), spread, preferred_element_type=F32)
    place = flat[0:1, :] * float(cap) + flat[1:2, :]
    gate = flat[2:3, :]
    gate_col = flat.T[:, 2:3]
    tile = min(256, slots)

    pl.semaphore_wait(barrier, nj + 1 + sum(jnp.where(mirrored(k) != z, 1, 0) for k in range(pieces)))

    def piece(k):
        return pl.ds(pl.multiple_of(k * thin, thin), thin)

    def placed(p, k):
        return pl.ds(pl.multiple_of(p * rows + k * thin, thin), thin)

    def fold_copy(k):
        return pltpu.make_async_remote_copy(
            src_ref=w_ref.at[piece(k), :], dst_ref=w_half.at[k], send_sem=t_ss.at[k], recv_sem=t_rs.at[k],
            device_id=(dp, mirrored(k) * 2 + core), device_id_type=MESH,
        )

    def enter_copy(k):
        return pltpu.make_async_remote_copy(
            src_ref=w_half.at[k], dst_ref=w_full.at[placed(dp, k), :], send_sem=u_ss.at[k], recv_sem=u_rs.at[k],
            device_id=(mirrored(k), z * 2 + core), device_id_type=MESH,
        )

    @pl.loop(0, pieces)
    def _(k):
        @pl.when(mirrored(k) != z)
        def _():
            fold_copy(k).start()

        @pl.when(mirrored(k) == z)
        def _():
            w_half[k] = w_ref[piece(k), :]

    @pl.loop(0, slots // tile)
    def _(i):
        here = pl.ds(pl.multiple_of(i * tile, tile), tile)
        slot = (lax.broadcasted_iota(jnp.int32, (tile, tok), 0) + i * tile).astype(F32)
        pick[here, :] = ((slot == place0).astype(F32) + (slot == place1).astype(F32)).astype(BF)
        slot = (lax.broadcasted_iota(jnp.int32, (tile, own), 0) + i * tile).astype(F32)
        chosen = (slot == place).astype(F32)
        flat_pick[here, :] = chosen.astype(BF)
        send_a[here, :] = jnp.dot(
            (chosen * gate).astype(BF), hid_ref[...], preferred_element_type=F32
        ).astype(BF)

    def act_copy(i):
        t, device = peer(i)
        return pltpu.make_async_remote_copy(
            src_ref=send_a.at[chunk(t), :], dst_ref=recv_a.at[chunk(j), :],
            send_sem=a_ss, recv_sem=a_rs, device_id=device, device_id_type=MESH,
        )

    def grad_copy(i, b):
        t, device = peer(i)
        return pltpu.make_async_remote_copy(
            src_ref=send_g.at[b, chunk(t), :], dst_ref=recv_g.at[b, chunk(j), :],
            send_sem=g_ss.at[b], recv_sem=g_rs.at[b], device_id=device, device_id_type=MESH,
        )

    def reply_copy(i):
        t, device = peer(i)
        return pltpu.make_async_remote_copy(
            src_ref=reply.at[chunk(t), :], dst_ref=back.at[chunk(j), :],
            send_sem=p_ss, recv_sem=p_rs, device_id=device, device_id_type=MESH,
        )

    most = pl.ds(0, slots - cap)

    def wait_rows(ref, sem):
        pltpu.make_async_copy(ref, ref, sem).wait()

    @pl.loop(0, nj - 1)
    def _(i):
        act_copy(i).start()

    recv_a[chunk(j), :] = send_a[chunk(j), :]

    def send_block(b):
        @pl.loop(0, slots // tile)
        def _(i):
            here = pl.ds(pl.multiple_of(i * tile, tile), tile)
            send_g[b, here, :] = jnp.dot(
                pick[here, :], grads_ref[:, b * db : (b + 1) * db], preferred_element_type=F32
            ).astype(BF)

        @pl.loop(0, nj - 1)
        def _(i):
            grad_copy(i, b).start()

        recv_g[b, chunk(j), :] = send_g[b, chunk(j), :]

    def ring_up(s, k):
        q = placed(entered(k, lax.rem(z - s + 1 + nz, nz)), k)
        return pltpu.make_async_remote_copy(
            src_ref=w_full.at[q, :], dst_ref=w_full.at[q, :], send_sem=gr_ss.at[s, k], recv_sem=gr_rs.at[s, k],
            device_id=up, device_id_type=MESH,
        )

    def ring_down(s, k):
        q = placed(entered(k, lax.rem(z + s - 1, nz)), k)
        return pltpu.make_async_remote_copy(
            src_ref=w_full.at[q, :], dst_ref=w_full.at[q, :], send_sem=gl_ss.at[s, k], recv_sem=gl_rs.at[s, k],
            device_id=down, device_id_type=MESH,
        )

    def gather_enter():
        @pl.loop(0, pieces)
        def _(k):
            @pl.when(mirrored(k) != z)
            def _():
                fold_copy(k).wait()

            @pl.when(mirrored(k) != dp)
            def _():
                enter_copy(k).start()

            @pl.when(mirrored(k) == dp)
            def _():
                w_full[placed(dp, k), :] = w_half[k]

    def gather_begin():
        @pl.loop(0, pieces)
        def _(k):
            @pl.when(mirrored(k) != dp)
            def _():
                enter_copy(k).wait()

            ring_up(1, k).start()
            if half > 1:
                ring_down(1, k).start()

    def gather_steps(first, last):
        @pl.loop(first, min(last, half - 1) + 1)
        def _(s):
            @pl.loop(0, pieces)
            def _(k):
                ring_up(s, k).wait_recv()
                ring_up(s + 1, k).start()
                ring_down(s, k).wait_recv()

                @pl.when(s + 1 < half)
                def _():
                    ring_down(s + 1, k).start()

        if last >= half:

            @pl.loop(0, pieces)
            def _(k):
                ring_up(half, k).wait_recv()

    def sum_up(s, b):
        return pltpu.make_async_remote_copy(
            src_ref=stage_r.at[b, s - 1], dst_ref=stage_r.at[b, s],
            send_sem=rr_ss.at[b, s], recv_sem=rr_rs.at[b, s], device_id=up, device_id_type=MESH,
        )

    def sum_down(s, b):
        return pltpu.make_async_remote_copy(
            src_ref=stage_l.at[b, s - 1], dst_ref=stage_l.at[b, s],
            send_sem=rl_ss.at[b, s], recv_sem=rl_rs.at[b, s], device_id=down, device_id_type=MESH,
        )

    def up_slice(s):
        return shard(lax.rem(z + half - s, nz))

    def down_slice(s):
        return shard(lax.rem(z - half - 1 + s + nz, nz))

    def leave_copy(b, k):
        return pltpu.make_async_remote_copy(
            src_ref=gfin.at[b, piece(k), :], dst_ref=g_half.at[b, k], send_sem=f_ss.at[b, k], recv_sem=f_rs.at[b, k],
            device_id=(entered(k, z), z * 2 + core), device_id_type=MESH,
        )

    def home_copy(b, k):
        return pltpu.make_async_remote_copy(
            src_ref=g_half.at[b, k], dst_ref=grad_ref.at[piece(k), b * db : (b + 1) * db],
            send_sem=h_ss.at[b, k], recv_sem=h_rs.at[b, k],
            device_id=(dp, mirrored(k) * 2 + core), device_id_type=MESH,
        )

    def home(b):
        @pl.loop(0, pieces)
        def _(k):
            @pl.when(entered(k, z) != dp)
            def _():
                leave_copy(b, k).wait()

            @pl.when(mirrored(k) != z)
            def _():
                home_copy(b, k).start()

            @pl.when(mirrored(k) == z)
            def _():
                grad_ref[piece(k), b * db : (b + 1) * db] = g_half[b, k]

    following = {}

    def sum_begin(b):
        stage_l[b, 0] = part[b, down_slice(1), :].astype(BF)
        sum_down(1, b).start()
        if half > 1:
            stage_r[b, 0] = part[b, up_slice(1), :].astype(BF)
            sum_up(1, b).start()
        following[b] = 1

    def sum_end(b):
        sum_down(half, b).wait_recv()
        total = part[b, shard(z), :] + stage_r[b, half - 1].astype(F32) + stage_l[b, half].astype(F32)
        gfin[b] = total.astype(BF)

        @pl.loop(0, pieces)
        def _(k):
            @pl.when(entered(k, z) != dp)
            def _():
                leave_copy(b, k).start()

            @pl.when(entered(k, z) == dp)
            def _():
                g_half[b, k] = gfin[b, piece(k), :]

        if b > 0:
            home(b - 1)

    def sum_steps(count):
        while count and following:
            n = min([count] + [half - s for s in following.values()])

            @pl.loop(0, n)
            def _(i):
                for b, first in following.items():
                    s = first + i
                    sum_down(s, b).wait_recv()
                    stage_l[b, s] = (stage_l[b, s].astype(F32) + part[b, down_slice(s + 1), :]).astype(BF)
                    sum_down(s + 1, b).start()
                    sum_up(s, b).wait_recv()

                    @pl.when(s + 1 < half)
                    def _():
                        stage_r[b, s] = (stage_r[b, s].astype(F32) + part[b, up_slice(s + 1), :]).astype(BF)
                        sum_up(s + 1, b).start()

            for b in list(following):
                following[b] += n
                if following[b] == half:
                    del following[b]
                    sum_end(b)
            count -= n

    wide = min(256, hid)

    def turn_acts():
        wait_rows(recv_a.at[most, :], a_rs)

        @pl.loop(0, hid // wide)
        def _(i):
            here = pl.ds(pl.multiple_of(i * wide, wide), wide)
            turned = recv_a[:, here].T
            for u in range(wide // thin):
                block = i * (wide // thin) + u
                k = lax.rem(block, pieces)
                q = lax.rem(block // pieces - dp + lag(k) + nz, nz)
                recv_at[placed(q, k), :] = turned[u * thin : (u + 1) * thin, :]

    def sum_block(b):
        wait_rows(recv_g.at[b, most, :], g_rs.at[b])

        @pl.loop(0, hid // wide)
        def _(i):
            here = pl.ds(pl.multiple_of(i * wide, wide), wide)
            part[b, here, :] = jnp.dot(recv_at[here, :], recv_g[b], preferred_element_type=F32)

        sum_begin(b)

    def reply_rows(i):
        here = slice(i * tile, (i + 1) * tile)
        reply[here, :] = sum(
            lax.dot_general(
                recv_g[b, here, :], w_full[:, b * db : (b + 1) * db], (((1,), (1,)), ((), ())),
                preferred_element_type=F32,
            )
            for b in range(nb)
        ).astype(BF)

    def gather_step(s):
        if s <= half:
            gather_steps(s, s)

    send_block(0)
    gather_enter()
    send_block(1)
    gather_begin()
    send_block(2)
    gather_step(1)
    send_block(3)
    gather_step(2)
    gather_step(3)
    turn_acts()
    gather_step(4)
    gather_step(5)
    gather_step(6)
    sum_block(0)
    gather_step(7)
    gather_step(8)
    sum_block(1)
    sum_block(2)
    sum_steps(1)
    sum_block(3)
    for i in range(slots // tile):
        reply_rows(i)
        sum_steps(1)

    @pl.loop(0, nj - 1)
    def _(i):
        reply_copy(i).start()

    back[chunk(j), :] = reply[chunk(j), :]
    sum_steps(half * nb)
    home(nb - 1)

    wait_rows(back.at[most, :], p_rs)
    row = lax.dot_general(flat_pick[...], back[...], (((0,), (0,)), ((), ())), preferred_element_type=F32)
    dh_ref[...] = (gate_col * row).astype(BF)
    sums = jnp.sum(hid_ref[...].astype(F32) * row, axis=1, keepdims=True)
    token = lax.broadcasted_iota(jnp.int32, (own, tok), 1) * 2
    slot = lax.broadcasted_iota(jnp.int32, (own, tok), 0)
    for k in range(2):
        gg_ref[k : k + 1, :] = jnp.sum(jnp.where(slot == token + k, sums, 0.0), axis=0, keepdims=True)

    wait_rows(send_a.at[most, :], a_ss)
    wait_rows(reply.at[most, :], p_ss)
    for b in range(nb):
        wait_rows(send_g.at[b, most, :], g_ss.at[b])

    @pl.loop(1, half)
    def _(s):
        @pl.loop(0, pieces)
        def _(k):
            ring_up(s, k).wait_send()
            ring_down(s, k).wait_send()

        @pl.loop(0, nb)
        def _(b):
            sum_up(s, b).wait_send()
            sum_down(s, b).wait_send()

    @pl.loop(0, pieces)
    def _(k):
        ring_up(half, k).wait_send()

    @pl.loop(0, nb)
    def _(b):
        sum_down(half, b).wait_send()

    for b in range(nb):

        @pl.loop(0, pieces)
        def _(k):
            @pl.when(mirrored(k) != z)
            def _():
                home_copy(b, k).wait()


def body(out_grad, hidden_act, expert_ids, gate_weight, down_weight, first_moment, second_moment):
    tok, top = expert_ids.shape
    width = out_grad.shape[1]
    hid = hidden_act.shape[2]
    nz = lax.axis_size("expert") // 2
    nj = 2 * lax.axis_size("dp")
    cap = 2 * tok * top // nj
    slots = nj * cap
    own = tok * top
    rows = hid // nz
    half = nz // 2
    nb = 4
    db = width // nb
    pieces = rows // 16
    dma = pltpu.SemaphoreType.DMA
    vmem = pl.BlockSpec(memory_space=pltpu.VMEM)
    dh, gg, gradient = pl.pallas_call(
        functools.partial(plane_kernel, (nz, nj, tok, cap, hid, nb, db, pieces)),
        out_shape=(
            jax.ShapeDtypeStruct((own, hid), BF),
            jax.ShapeDtypeStruct((top, tok), F32),
            jax.ShapeDtypeStruct((rows, width), BF),
        ),
        in_specs=[vmem] * 5,
        out_specs=(vmem,) * 3,
        scratch_shapes=[
            pltpu.VMEM((slots, tok), BF),
            pltpu.VMEM((slots, own), BF),
            pltpu.VMEM((slots, hid), BF),
            pltpu.VMEM((nb, slots, db), BF),
            pltpu.VMEM((slots, hid), BF),
            pltpu.VMEM((hid, slots), BF),
            pltpu.VMEM((nb, slots, db), BF),
            pltpu.VMEM((hid, width), BF),
            pltpu.VMEM((nb, hid, db), F32),
            pltpu.VMEM((slots, hid), BF),
            pltpu.VMEM((slots, hid), BF),
            pltpu.VMEM((nb, half, rows, db), BF),
            pltpu.VMEM((nb, half + 1, rows, db), BF),
            pltpu.VMEM((nb, rows, db), BF),
            pltpu.VMEM((pieces, rows // pieces, width), BF),
            pltpu.VMEM((nb, pieces, rows // pieces, db), BF),
            dma, dma, dma((nb,)), dma((nb,)), dma, dma,
            dma((pieces,)), dma((pieces,)), dma((pieces,)), dma((pieces,)),
            dma((half + 1, pieces)), dma((half + 1, pieces)), dma((half + 1, pieces)), dma((half + 1, pieces)),
            dma((nb, half + 1)), dma((nb, half + 1)), dma((nb, half + 1)), dma((nb, half + 1)),
            dma((nb, pieces)), dma((nb, pieces)), dma((nb, pieces)), dma((nb, pieces)),
        ],
        compiler_params=pltpu.CompilerParams(
            collective_id=0, has_side_effects=True, vmem_limit_bytes=58 * 1024 * 1024
        ),
    )(
        out_grad, hidden_act.reshape(own, hid), expert_ids.T, gate_weight.T, down_weight[0],
    )
    gradient = gradient.astype(F32)
    moment_new = beta_one * first_moment[0] + (1.0 - beta_one) * gradient
    second_new = beta_two * second_moment[0] + (1.0 - beta_two) * gradient * gradient
    fix_one = 1.0 - beta_one**STEP
    fix_two = 1.0 - beta_two**STEP
    update = moment_new / fix_one / (jnp.sqrt(second_new / fix_two) + adam_eps)
    return dh.reshape(tok, top, hid), gg.T, moment_new[None], second_new[None], update[None]


def solution(mesh):
    return jax.shard_map(
        body,
        mesh=mesh,
        in_specs=(
            P(("dp", "expert"), None),
            P(("dp", "expert"), None, None),
            P(("dp", "expert"), None),
            P(("dp", "expert"), None),
            P("expert", "dp", None),
            P("expert", "dp", None),
            P("expert", "dp", None),
        ),
        out_specs=(
            P(("dp", "expert"), None, None),
            P(("dp", "expert"), None),
            P("expert", "dp", None),
            P("expert", "dp", None),
            P("expert", "dp", None),
        ),
        check_vma=False,
    )
```

```python
import functools

import jax
import jax.numpy as jnp
from jax import lax
from jax.experimental import pallas as pl
from jax.experimental.pallas import tpu as pltpu
from jax.sharding import PartitionSpec as P

STEP = 11
MESH = pl.DeviceIdType.MESH
BF = jnp.bfloat16
F32 = jnp.float32

beta_one = 0.9
beta_two = 0.999
adam_eps = 1e-08


def plane_kernel(
    sizes, grads_ref, hid_ref, ids_ref, gate_ref, w_ref,
    dh_ref, gg_ref, grad_ref,
    pick, flat_pick, send_a, send_g, recv_a, recv_at, recv_g, w_full, part, reply, back,
    stage_r, stage_l, gfin, w_half, g_half,
    a_ss, a_rs, g_ss, g_rs, p_ss, p_rs, t_ss, t_rs, u_ss, u_rs, gr_ss, gr_rs, gl_ss, gl_rs,
    rr_ss, rr_rs, rl_ss, rl_rs, f_ss, f_rs, h_ss, h_rs,
):
    nz, nj, tok, cap, hid, nb, db, pieces = sizes
    half = nz // 2
    rows = hid // nz
    thin = rows // pieces
    slots = nj * cap
    own = 2 * tok
    dp = lax.axis_index("dp")
    ez = lax.axis_index("expert")
    z = ez // 2
    core = lax.rem(ez, 2)
    j = dp * 2 + core
    z_up, z_down = lax.rem(z + 1, nz), lax.rem(z + nz - 1, nz)
    up, down = (dp, z_up * 2 + core), (dp, z_down * 2 + core)

    def lag(k):
        return k * nz // pieces

    def mirrored(k):
        return lax.rem(dp + lag(k) - z + nz, nz)

    def entered(k, q):
        return lax.rem(dp + q - lag(k) + 2 * nz, nz)

    def peer(i):
        if nj != 32:
            t = lax.rem(j + i + 1, nj)
            return t, (t // 2, z * 2 + lax.rem(t, 2))
        turn = lax.rem(i, 4)
        cos = (1 - turn) * (1 - lax.rem(turn, 2))
        sin = (2 - turn) * lax.rem(turn, 2)
        reach = lax.rem(i // 4, 3)
        early = i < 24
        rest = 3 - turn
        dy = jnp.where(early, reach * cos + sin, 2 * (rest // 2))
        dx = jnp.where(early, cos - reach * sin, 2 * lax.rem(rest, 2))
        dc = jnp.where(early, 1 - i // 12, 1 - (i - 24) // 4)
        mirror = 1 - 2 * core
        y = lax.rem(dp // 4 + mirror * dy + 4, 4)
        x = lax.rem(lax.rem(dp, 4) + mirror * dx + 4, 4)
        c = lax.rem(core + dc, 2)
        return (y * 4 + x) * 2 + c, (y * 4 + x, z * 2 + c)

    def chunk(t):
        return pl.ds(pl.multiple_of(t * cap, cap), cap)

    def shard(q):
        return pl.ds(pl.multiple_of(q * rows, rows), rows)

    barrier = pltpu.get_barrier_semaphore()

    @pl.loop(0, nj - 1)
    def _(i):
        pl.semaphore_signal(barrier, inc=1, device_id=peer(i)[1], device_id_type=MESH)

    pl.semaphore_signal(barrier, inc=1, device_id=up, device_id_type=MESH)
    pl.semaphore_signal(barrier, inc=1, device_id=down, device_id_type=MESH)

    for k in range(pieces):

        @pl.when(mirrored(k) != z)
        def _():
            across = (dp, mirrored(k) * 2 + core)
            pl.semaphore_signal(barrier, inc=1, device_id=across, device_id_type=MESH)

    experts = lax.broadcasted_iota(jnp.int32, (nj, tok), 0)
    hot0 = (experts == ids_ref[0:1, :]).astype(F32)
    hot1 = (experts == ids_ref[1:2, :]).astype(F32)
    before = (
        lax.broadcasted_iota(jnp.int32, (tok, tok), 0)
        < lax.broadcasted_iota(jnp.int32, (tok, tok), 1)
    ).astype(F32).astype(BF)
    run0 = jnp.dot(hot0.astype(BF), before, preferred_element_type=F32)
    run1 = jnp.dot(hot1.astype(BF), before, preferred_element_type=F32)
    run1 = run1 + jnp.sum(hot0, axis=1, keepdims=True)
    rank0 = jnp.sum(hot0 * run0, axis=0, keepdims=True)
    rank1 = jnp.sum(hot1 * run1, axis=0, keepdims=True)
    place0 = ids_ref[0:1, :].astype(F32) * float(cap) + rank0
    place1 = ids_ref[1:2, :].astype(F32) * float(cap) + rank1
    blank = jnp.zeros((5, tok), F32)
    token = lax.broadcasted_iota(jnp.int32, (tok, own), 0) * 2
    slot = lax.broadcasted_iota(jnp.int32, (tok, own), 1)
    flat = jnp.zeros((8, own), F32)
    for k, rank in enumerate((rank0, rank1)):
        facts = jnp.concatenate(
            [ids_ref[k : k + 1, :].astype(F32), rank, gate_ref[k : k + 1, :].astype(F32), blank], axis=0
        )
        spread = (slot == token + k).astype(F32).astype(BF)
        flat = flat + jnp.dot(facts.astype(BF), spread, preferred_element_type=F32)
    place = flat[0:1, :] * float(cap) + flat[1:2, :]
    gate = flat[2:3, :]
    gate_col = flat.T[:, 2:3]
    tile = min(256, slots)

    pl.semaphore_wait(barrier, nj + 1 + sum(jnp.where(mirrored(k) != z, 1, 0) for k in range(pieces)))

    def piece(k):
        return pl.ds(pl.multiple_of(k * thin, thin), thin)

    def placed(p, k):
        return pl.ds(pl.multiple_of(p * rows + k * thin, thin), thin)

    def fold_copy(k):
        return pltpu.make_async_remote_copy(
            src_ref=w_ref.at[piece(k), :], dst_ref=w_half.at[k], send_sem=t_ss.at[k], recv_sem=t_rs.at[k],
            device_id=(dp, mirrored(k) * 2 + core), device_id_type=MESH,
        )

    def enter_copy(k):
        return pltpu.make_async_remote_copy(
            src_ref=w_half.at[k], dst_ref=w_full.at[placed(dp, k), :], send_sem=u_ss.at[k], recv_sem=u_rs.at[k],
            device_id=(mirrored(k), z * 2 + core), device_id_type=MESH,
        )

    @pl.loop(0, pieces)
    def _(k):
        @pl.when(mirrored(k) != z)
        def _():
            fold_copy(k).start()

        @pl.when(mirrored(k) == z)
        def _():
            w_half[k] = w_ref[piece(k), :]

    @pl.loop(0, slots // tile)
    def _(i):
        here = pl.ds(pl.multiple_of(i * tile, tile), tile)
        slot = (lax.broadcasted_iota(jnp.int32, (tile, tok), 0) + i * tile).astype(F32)
        pick[here, :] = ((slot == place0).astype(F32) + (slot == place1).astype(F32)).astype(BF)
        slot = (lax.broadcasted_iota(jnp.int32, (tile, own), 0) + i * tile).astype(F32)
        chosen = (slot == place).astype(F32)
        flat_pick[here, :] = chosen.astype(BF)
        send_a[here, :] = jnp.dot(
            (chosen * gate).astype(BF), hid_ref[...], preferred_element_type=F32
        ).astype(BF)

    def act_copy(i):
        t, device = peer(i)
        return pltpu.make_async_remote_copy(
            src_ref=send_a.at[chunk(t), :], dst_ref=recv_a.at[chunk(j), :],
            send_sem=a_ss, recv_sem=a_rs, device_id=device, device_id_type=MESH,
        )

    def grad_copy(i, b):
        t, device = peer(i)
        return pltpu.make_async_remote_copy(
            src_ref=send_g.at[b, chunk(t), :], dst_ref=recv_g.at[b, chunk(j), :],
            send_sem=g_ss.at[b], recv_sem=g_rs.at[b], device_id=device, device_id_type=MESH,
        )

    def reply_copy(i):
        t, device = peer(i)
        return pltpu.make_async_remote_copy(
            src_ref=reply.at[chunk(t), :], dst_ref=back.at[chunk(j), :],
            send_sem=p_ss, recv_sem=p_rs, device_id=device, device_id_type=MESH,
        )

    most = pl.ds(0, slots - cap)

    def wait_rows(ref, sem):
        pltpu.make_async_copy(ref, ref, sem).wait()

    @pl.loop(0, nj - 1)
    def _(i):
        act_copy(i).start()

    recv_a[chunk(j), :] = send_a[chunk(j), :]

    def send_block(b):
        @pl.loop(0, slots // tile)
        def _(i):
            here = pl.ds(pl.multiple_of(i * tile, tile), tile)
            send_g[b, here, :] = jnp.dot(
                pick[here, :], grads_ref[:, b * db : (b + 1) * db], preferred_element_type=F32
            ).astype(BF)

        @pl.loop(0, nj - 1)
        def _(i):
            grad_copy(i, b).start()

        recv_g[b, chunk(j), :] = send_g[b, chunk(j), :]

    def ring_up(s, k):
        q = placed(entered(k, lax.rem(z - s + 1 + nz, nz)), k)
        return pltpu.make_async_remote_copy(
            src_ref=w_full.at[q, :], dst_ref=w_full.at[q, :], send_sem=gr_ss.at[s, k], recv_sem=gr_rs.at[s, k],
            device_id=up, device_id_type=MESH,
        )

    def ring_down(s, k):
        q = placed(entered(k, lax.rem(z + s - 1, nz)), k)
        return pltpu.make_async_remote_copy(
            src_ref=w_full.at[q, :], dst_ref=w_full.at[q, :], send_sem=gl_ss.at[s, k], recv_sem=gl_rs.at[s, k],
            device_id=down, device_id_type=MESH,
        )

    def gather_enter():
        @pl.loop(0, pieces)
        def _(k):
            @pl.when(mirrored(k) != z)
            def _():
                fold_copy(k).wait()

            @pl.when(mirrored(k) != dp)
            def _():
                enter_copy(k).start()

            @pl.when(mirrored(k) == dp)
            def _():
                w_full[placed(dp, k), :] = w_half[k]

    def gather_begin():
        @pl.loop(0, pieces)
        def _(k):
            @pl.when(mirrored(k) != dp)
            def _():
                enter_copy(k).wait()

            ring_up(1, k).start()
            if half > 1:
                ring_down(1, k).start()

    def gather_steps(first, last):
        @pl.loop(first, min(last, half - 1) + 1)
        def _(s):
            @pl.loop(0, pieces)
            def _(k):
                ring_up(s, k).wait_recv()
                ring_up(s + 1, k).start()
                ring_down(s, k).wait_recv()

                @pl.when(s + 1 < half)
                def _():
                    ring_down(s + 1, k).start()

        if last >= half:

            @pl.loop(0, pieces)
            def _(k):
                ring_up(half, k).wait_recv()

    def sum_up(s, b):
        return pltpu.make_async_remote_copy(
            src_ref=stage_r.at[b, s - 1], dst_ref=stage_r.at[b, s],
            send_sem=rr_ss.at[b, s], recv_sem=rr_rs.at[b, s], device_id=up, device_id_type=MESH,
        )

    def sum_down(s, b):
        return pltpu.make_async_remote_copy(
            src_ref=stage_l.at[b, s - 1], dst_ref=stage_l.at[b, s],
            send_sem=rl_ss.at[b, s], recv_sem=rl_rs.at[b, s], device_id=down, device_id_type=MESH,
        )

    def up_slice(s):
        return shard(lax.rem(z + half - s, nz))

    def down_slice(s):
        return shard(lax.rem(z - half - 1 + s + nz, nz))

    def leave_copy(b, k):
        return pltpu.make_async_remote_copy(
            src_ref=gfin.at[b, piece(k), :], dst_ref=g_half.at[b, k], send_sem=f_ss.at[b, k], recv_sem=f_rs.at[b, k],
            device_id=(entered(k, z), z * 2 + core), device_id_type=MESH,
        )

    def home_copy(b, k):
        return pltpu.make_async_remote_copy(
            src_ref=g_half.at[b, k], dst_ref=grad_ref.at[piece(k), b * db : (b + 1) * db],
            send_sem=h_ss.at[b, k], recv_sem=h_rs.at[b, k],
            device_id=(dp, mirrored(k) * 2 + core), device_id_type=MESH,
        )

    def home(b):
        @pl.loop(0, pieces)
        def _(k):
            @pl.when(entered(k, z) != dp)
            def _():
                leave_copy(b, k).wait()

            @pl.when(mirrored(k) != z)
            def _():
                home_copy(b, k).start()

            @pl.when(mirrored(k) == z)
            def _():
                grad_ref[piece(k), b * db : (b + 1) * db] = g_half[b, k]

    following, leaving = {}, []

    def sum_begin(b):
        stage_l[b, 0] = part[b, down_slice(1), :].astype(BF)
        sum_down(1, b).start()
        if half > 1:
            stage_r[b, 0] = part[b, up_slice(1), :].astype(BF)
            sum_up(1, b).start()
        following[b] = 1

    def sum_end(b):
        sum_down(half, b).wait_recv()
        total = part[b, shard(z), :] + stage_r[b, half - 1].astype(F32) + stage_l[b, half].astype(F32)
        gfin[b] = total.astype(BF)

        @pl.loop(0, pieces)
        def _(k):
            @pl.when(entered(k, z) != dp)
            def _():
                leave_copy(b, k).start()

            @pl.when(entered(k, z) == dp)
            def _():
                g_half[b, k] = gfin[b, piece(k), :]

    def sum_steps(count):
        while count and following:
            n = min([count] + [half - s for s in following.values()])

            @pl.loop(0, n)
            def _(i):
                for b, first in following.items():
                    s = first + i
                    sum_down(s, b).wait_recv()
                    stage_l[b, s] = (stage_l[b, s].astype(F32) + part[b, down_slice(s + 1), :]).astype(BF)
                    sum_down(s + 1, b).start()
                    sum_up(s, b).wait_recv()

                    @pl.when(s + 1 < half)
                    def _():
                        stage_r[b, s] = (stage_r[b, s].astype(F32) + part[b, up_slice(s + 1), :]).astype(BF)
                        sum_up(s + 1, b).start()

            while leaving:
                home(leaving.pop(0))
            for b in list(following):
                following[b] += n
                if following[b] == half:
                    del following[b]
                    sum_end(b)
                    leaving.append(b)
            count -= n

    wide = min(256, hid)

    def turn_acts():
        wait_rows(recv_a.at[most, :], a_rs)

        @pl.loop(0, hid // wide)
        def _(i):
            here = pl.ds(pl.multiple_of(i * wide, wide), wide)
            turned = recv_a[:, here].T
            for u in range(wide // thin):
                block = i * (wide // thin) + u
                k = lax.rem(block, pieces)
                q = lax.rem(block // pieces - dp + lag(k) + nz, nz)
                recv_at[placed(q, k), :] = turned[u * thin : (u + 1) * thin, :]

    def sum_block(b):
        wait_rows(recv_g.at[b, most, :], g_rs.at[b])

        @pl.loop(0, hid // wide)
        def _(i):
            here = pl.ds(pl.multiple_of(i * wide, wide), wide)
            part[b, here, :] = jnp.dot(recv_at[here, :], recv_g[b], preferred_element_type=F32)

        sum_begin(b)

    def reply_rows(i):
        here = slice(i * tile, (i + 1) * tile)
        reply[here, :] = sum(
            lax.dot_general(
                recv_g[b, here, :], w_full[:, b * db : (b + 1) * db], (((1,), (1,)), ((), ())),
                preferred_element_type=F32,
            )
            for b in range(nb)
        ).astype(BF)

    def gather_step(s):
        if s <= half:
            gather_steps(s, s)

    send_block(0)
    gather_enter()
    send_block(1)
    gather_begin()
    send_block(2)
    gather_step(1)
    send_block(3)
    gather_step(2)
    gather_step(3)
    turn_acts()
    gather_step(4)
    gather_step(5)
    gather_step(6)
    sum_block(0)
    gather_step(7)
    gather_step(8)
    sum_block(1)
    sum_block(2)
    sum_steps(1)
    sum_block(3)
    for i in range(slots // tile):
        reply_rows(i)
        sum_steps(1)

    @pl.loop(0, nj - 1)
    def _(i):
        reply_copy(i).start()

    back[chunk(j), :] = reply[chunk(j), :]
    sum_steps(half * nb)

    wait_rows(back.at[most, :], p_rs)
    row = lax.dot_general(flat_pick[...], back[...], (((0,), (0,)), ((), ())), preferred_element_type=F32)
    dh_ref[...] = (gate_col * row).astype(BF)
    while leaving:
        home(leaving.pop(0))
    sums = jnp.sum(hid_ref[...].astype(F32) * row, axis=1, keepdims=True)
    token = lax.broadcasted_iota(jnp.int32, (own, tok), 1) * 2
    slot = lax.broadcasted_iota(jnp.int32, (own, tok), 0)
    for k in range(2):
        gg_ref[k : k + 1, :] = jnp.sum(jnp.where(slot == token + k, sums, 0.0), axis=0, keepdims=True)

    wait_rows(send_a.at[most, :], a_ss)
    wait_rows(reply.at[most, :], p_ss)
    for b in range(nb):
        wait_rows(send_g.at[b, most, :], g_ss.at[b])

    @pl.loop(1, half)
    def _(s):
        @pl.loop(0, pieces)
        def _(k):
            ring_up(s, k).wait_send()
            ring_down(s, k).wait_send()

        @pl.loop(0, nb)
        def _(b):
            sum_up(s, b).wait_send()
            sum_down(s, b).wait_send()

    @pl.loop(0, pieces)
    def _(k):
        ring_up(half, k).wait_send()

    @pl.loop(0, nb)
    def _(b):
        sum_down(half, b).wait_send()

    for b in range(nb):

        @pl.loop(0, pieces)
        def _(k):
            @pl.when(mirrored(k) != z)
            def _():
                home_copy(b, k).wait()


def body(out_grad, hidden_act, expert_ids, gate_weight, down_weight, first_moment, second_moment):
    tok, top = expert_ids.shape
    width = out_grad.shape[1]
    hid = hidden_act.shape[2]
    nz = lax.axis_size("expert") // 2
    nj = 2 * lax.axis_size("dp")
    cap = 2 * tok * top // nj
    slots = nj * cap
    own = tok * top
    rows = hid // nz
    half = nz // 2
    nb = 4
    db = width // nb
    pieces = rows // 16
    dma = pltpu.SemaphoreType.DMA
    vmem = pl.BlockSpec(memory_space=pltpu.VMEM)
    dh, gg, gradient = pl.pallas_call(
        functools.partial(plane_kernel, (nz, nj, tok, cap, hid, nb, db, pieces)),
        out_shape=(
            jax.ShapeDtypeStruct((own, hid), BF),
            jax.ShapeDtypeStruct((top, tok), F32),
            jax.ShapeDtypeStruct((rows, width), BF),
        ),
        in_specs=[vmem] * 5,
        out_specs=(vmem,) * 3,
        scratch_shapes=[
            pltpu.VMEM((slots, tok), BF),
            pltpu.VMEM((slots, own), BF),
            pltpu.VMEM((slots, hid), BF),
            pltpu.VMEM((nb, slots, db), BF),
            pltpu.VMEM((slots, hid), BF),
            pltpu.VMEM((hid, slots), BF),
            pltpu.VMEM((nb, slots, db), BF),
            pltpu.VMEM((hid, width), BF),
            pltpu.VMEM((nb, hid, db), F32),
            pltpu.VMEM((slots, hid), BF),
            pltpu.VMEM((slots, hid), BF),
            pltpu.VMEM((nb, half, rows, db), BF),
            pltpu.VMEM((nb, half + 1, rows, db), BF),
            pltpu.VMEM((nb, rows, db), BF),
            pltpu.VMEM((pieces, rows // pieces, width), BF),
            pltpu.VMEM((nb, pieces, rows // pieces, db), BF),
            dma, dma, dma((nb,)), dma((nb,)), dma, dma,
            dma((pieces,)), dma((pieces,)), dma((pieces,)), dma((pieces,)),
            dma((half + 1, pieces)), dma((half + 1, pieces)), dma((half + 1, pieces)), dma((half + 1, pieces)),
            dma((nb, half + 1)), dma((nb, half + 1)), dma((nb, half + 1)), dma((nb, half + 1)),
            dma((nb, pieces)), dma((nb, pieces)), dma((nb, pieces)), dma((nb, pieces)),
        ],
        compiler_params=pltpu.CompilerParams(
            collective_id=0, has_side_effects=True, vmem_limit_bytes=58 * 1024 * 1024
        ),
    )(
        out_grad, hidden_act.reshape(own, hid), expert_ids.T, gate_weight.T, down_weight[0],
    )
    gradient = gradient.astype(F32)
    moment_new = beta_one * first_moment[0] + (1.0 - beta_one) * gradient
    second_new = beta_two * second_moment[0] + (1.0 - beta_two) * gradient * gradient
    fix_one = 1.0 - beta_one**STEP
    fix_two = 1.0 - beta_two**STEP
    update = moment_new / fix_one / (jnp.sqrt(second_new / fix_two) + adam_eps)
    return dh.reshape(tok, top, hid), gg.T, moment_new[None], second_new[None], update[None]


def solution(mesh):
    return jax.shard_map(
        body,
        mesh=mesh,
        in_specs=(
            P(("dp", "expert"), None),
            P(("dp", "expert"), None, None),
            P(("dp", "expert"), None),
            P(("dp", "expert"), None),
            P("expert", "dp", None),
            P("expert", "dp", None),
            P("expert", "dp", None),
        ),
        out_specs=(
            P(("dp", "expert"), None, None),
            P(("dp", "expert"), None),
            P("expert", "dp", None),
            P("expert", "dp", None),
            P("expert", "dp", None),
        ),
        check_vma=False,
    )
```
